1024 devices in a mesh: rep: 4 (over z_hi, core), fsdp: 256 (over x, y, z_lo).
Axes of the slice: x: 8, y: 8, z: 8 (z_hi: 2, z_lo: 4; z = z_hi * 4 + z_lo), core: 2. Of those that a mesh axis runs over, the one named last changes fastest.
Arguments:
- tokens: bfloat16 [4, 32768, 8192], P('rep', 'fsdp'), may hold values from -6 to 6
- local_weights: bfloat16 [4, 10, 256, 8192], P('rep', None, 'fsdp'), may hold values from -6 to 6
- base_weights: bfloat16 [10, 256, 8192], P(None, 'fsdp'), may hold values from -6 to 6
- momentum: float32 [10, 256, 8192], P(None, 'fsdp'), may hold values from -6 to 6
Outputs:
- projected: bfloat16 [4, 32768, 256], P('rep', 'fsdp')
- new_base: bfloat16 [10, 256, 8192], P(None, 'fsdp')
- new_momentum: float32 [10, 256, 8192], P(None, 'fsdp')
- new_local: bfloat16 [4, 10, 256, 8192], P('rep', None, 'fsdp')
The draws below stay inside these ranges and needn't reach their ends.
All inputs are finite; a program needn't handle non-finite values.
Results may differ from the reference program's by a relative error of at most 0.02.
Values may be sent and summed in bfloat16 or wider, within the bound.
A program may use at most 64 MiB of HBM per device.

```python
import math
import jax
import jax.numpy as jnp
from jax import lax

D = 8192
LAYERS = 10
ROWS = 256
TOKENS = 32768
N_REP = 4


def block_levels(stream_key, extent, pieces, least, high):
    def one(axis_at, parts):
        heights = jax.random.uniform(jax.random.fold_in(jax.random.fold_in(stream_key, 6), axis_at), (parts,), jnp.float32, least / len(pieces), high / len(pieces))
        return jnp.repeat(jnp.exp(heights), extent[axis_at] // parts).reshape((-1,) + (1,) * (len(extent) - axis_at - 1))

    loudness = one(*pieces[0])
    for cut in pieces[1:]:
        loudness = loudness * one(*cut)
    return loudness


def gaussian(key, dims, scale, most, split=(), held_as=jnp.bfloat16):
    factor_of = block_levels(key, dims, split, -0.22, 0.18) if split else 1.0
    array = jax.random.normal(key, dims, jnp.float32) * scale * factor_of
    return jnp.minimum(jnp.maximum(array, -most), most).astype(held_as)


def setup_inputs(seed: int = 0) -> dict:
    key_list = jax.random.split(jax.random.key(seed), 5)
    tokens = gaussian(key_list[0], (N_REP, TOKENS, D), 1.0, 6.0, ((0, 4), (1, 256)))
    local_weights = gaussian(key_list[1], (N_REP, LAYERS, ROWS, D), 1.0, 6.0, ((0, 4), (2, 256)))
    base_weights = gaussian(key_list[2], (LAYERS, ROWS, D), 1.0, 6.0, ((1, 256),))
    momentum = gaussian(key_list[3], (LAYERS, ROWS, D), 1.0, 6.0, ((1, 256),), jnp.float32)
    return {"tokens": tokens, "local_weights": local_weights, "base_weights": base_weights, "momentum": momentum}


def reference(tokens, local_weights, base_weights, momentum):
    factor = 1.0 / math.sqrt(D)

    def project(pair):
        return (jnp.dot(pair[0], pair[1].T, preferred_element_type=jnp.float32) * factor).astype(jnp.bfloat16)
    projected = lax.map(project, (tokens, local_weights[:, 0]))
    base_wide = base_weights.astype(jnp.float32)
    coded_delta = (base_wide[None] - local_weights.astype(jnp.float32)).astype(jnp.bfloat16)
    widened = lax.optimization_barrier(coded_delta).astype(jnp.float32)
    average = lax.optimization_barrier(jnp.sum(widened, axis=0)) / N_REP
    outer_grad = average.astype(jnp.bfloat16)
    outer_wide = lax.optimization_barrier(outer_grad).astype(jnp.float32)
    new_momentum = 0.9 * momentum + outer_wide
    new_base = (base_wide - 0.7 * (outer_wide + 0.9 * new_momentum)).astype(jnp.bfloat16)
    base_again = lax.optimization_barrier(new_base).astype(jnp.float32)
    new_local = (0.5 * local_weights.astype(jnp.float32) + 0.5 * base_again[None]).astype(jnp.bfloat16)
    return (projected, new_base, new_momentum, new_local)
```

```python
import functools
import math

import jax
import jax.numpy as jnp
from jax import lax
from jax.experimental import pallas as pl
from jax.experimental.pallas import tpu as pltpu
from jax.sharding import PartitionSpec as P

LANES = 128
MESH = pl.DeviceIdType.MESH
NT = (((1,), (1,)), ((), ()))


class Sizes:
    def __init__(self, x, y, z, width, layers, tokens, chunks):
        self.x, self.y, self.z = x, y, z
        self.width, self.layers, self.tokens, self.chunks = width, layers, tokens, chunks
        self.rows = x * y * z
        self.half = width // 2
        self.cols = self.half // chunks
        self.groups = self.half // LANES


def kernel(
    n,
    tok_hbm, loc_hbm, base_hbm, mom_hbm,
    proj_out, base_out, mom_out, local_out,
    tok, loc, base, mom, row, zbuf, plane, wide, ring_a, ring_b, delta, pair, cross, outer,
    load_sem, z_send, z_recv, p_send, p_recv, r_send, r_recv, d_send, d_recv,
):
    rep, me = lax.axis_index("rep"), lax.axis_index("fsdp")
    x, y, z = me // (n.y * n.z), (me // n.z) % n.y, me % n.z

    def at(x_, y_, z_):
        return {"fsdp": (x_ * n.y + y_) * n.z + z_}

    sibling = {"rep": rep + 1 - 2 * (rep % 2)}
    far = {"rep": lax.rem(rep + 2, 4)}

    def x_peer(k):
        return at(lax.rem(x + k, n.x), y, z)

    def y_peer(k):
        return at(x, lax.rem(y + k, n.y), z)

    def z_peer(k):
        return at(x, y, lax.rem(z + k, n.z))

    loads = [
        pltpu.make_async_copy(src, dst, load_sem.at[i])
        for i, (src, dst) in enumerate(((loc_hbm, loc), (base_hbm, base), (mom_hbm, mom), (tok_hbm, tok)))
    ]
    for load in loads:
        load.start()

    barrier = pltpu.get_barrier_semaphore()
    peers = (
        [sibling, far]
        + [z_peer(k) for k in range(1, n.z)]
        + [x_peer(k) for k in range(1, n.x)]
        + [y_peer(k) for k in range(1, n.y)]
    )
    for peer in peers:
        pl.semaphore_signal(barrier, inc=1, device_id=peer, device_id_type=MESH)

    def copy(src, dst, send, recv, peer):
        return pltpu.make_async_remote_copy(
            src_ref=src, dst_ref=dst, send_sem=send, recv_sem=recv, device_id=peer, device_id_type=MESH
        )

    sent = []

    def start(*args):
        c = copy(*args)
        c.start()
        sent.append(c)

    loads[0].wait()
    first = loc[0:1, :].astype(jnp.float32)
    for g in range(2 * n.groups):
        row[g : g + 1, :] = first[:, g * LANES : (g + 1) * LANES]
    for part in range(2):
        zbuf[part, z] = row[part * n.groups : (part + 1) * n.groups, :].astype(jnp.bfloat16)

    with jax.named_scope("entry_barrier"):
        pl.semaphore_wait(barrier, len(peers))

    for k in range(1, n.z):
        start(zbuf.at[:, z], zbuf.at[:, z], z_send.at[k], z_recv.at[k], z_peer(k))

    loads[1].wait()
    delta[...] = jnp.zeros_like(delta)
    delta[:, 0 : n.layers, :] = jnp.stack(
        [
            (
                base[:, h * n.half : (h + 1) * n.half].astype(jnp.float32)
                - loc[:, h * n.half : (h + 1) * n.half].astype(jnp.float32)
            ).astype(jnp.bfloat16)
            for h in range(2)
        ]
    )
    mine = rep % 2
    start(delta.at[1 - mine], pair, d_send.at[0], d_recv.at[0], sibling)

    with jax.named_scope("z_wait"):
        for k in range(1, n.z):
            slot = lax.rem(z - k + n.z, n.z)
            copy(zbuf.at[:, slot], zbuf.at[:, slot], z_send.at[k], z_recv.at[k], z_peer(k)).wait_recv()

    for k in range(1, max(n.x, n.y)):
        if k < n.x:
            start(zbuf.at[0], plane.at[0, x], p_send.at[0, k], p_recv.at[0, k], x_peer(k))
        if k < n.y:
            start(zbuf.at[1], plane.at[1, y], p_send.at[1, k], p_recv.at[1, k], y_peer(k))
    plane[0, x] = zbuf[0]
    plane[1, y] = zbuf[1]

    with jax.named_scope("pair_sum"):
        copy(pair, pair, d_send.at[0], d_recv.at[0], sibling).wait_recv()
        total = delta[mine].astype(jnp.float32) + pair[...].astype(jnp.float32)
        cross[0] = total.astype(jnp.bfloat16)
        start(cross.at[0], cross.at[1], d_send.at[1], d_recv.at[1], far)

    rings = ((ring_a, y, n.y, y_peer, x, n.x), (ring_b, x, n.x, x_peer, y, n.y))

    def block_rows(part):
        return rings[part][5] * n.z

    def hop(part, c, way, s, inward):
        ring, p, size, peer, _, _ = rings[part]
        rows = block_rows(part)
        block = lax.rem(p - (s - 1) + size, size) if way == 0 else lax.rem(p + (s - 1), size)
        got = lax.rem(p - s + size, size) if way == 0 else lax.rem(p + s, size)
        to = peer(1) if way == 0 else peer(size - 1)
        cut = pl.ds(0, rows)
        if s == size // 2:
            cut = pl.ds(0, rows // 2) if way == 0 else pl.ds(rows // 2, rows // 2)
        sems = (r_send.at[part, c, way, s - 1], r_recv.at[part, c, way, s - 1])
        slot = ring.at[c, got if inward else block, cut]
        return copy(slot, slot, *sems, to)

    def go(part, c, way, s):
        sent.append(hop(part, c, way, s, False))
        sent[-1].start()

    def arrived(part, c, way, s):
        hop(part, c, way, s, True).wait_recv()

    for part in range(2):
        ring, p, _, _, other, count = rings[part]
        with jax.named_scope("plane_wait"):
            for k in range(1, count):
                slot = lax.rem(other - k + count, count)
                copy(
                    plane.at[part, slot], plane.at[part, slot], p_send.at[part, k], p_recv.at[part, k], sibling
                ).wait_recv()
        with jax.named_scope("relayout"):
            rows = block_rows(part)
            wide[0 : rows * n.groups, :] = (
                plane[part, 0:count].reshape(rows * n.groups, LANES).astype(jnp.float32)
            )
            per = n.cols // LANES
            for c in range(n.chunks):
                for i in range(per):
                    ring[c, p, :, i * LANES : (i + 1) * LANES] = wide[
                        pl.ds(c * per + i, rows, stride=n.groups), :
                    ].astype(jnp.bfloat16)
                for way in range(2):
                    go(part, c, way, 1)

    def average():
        with jax.named_scope("average"):
            copy(cross.at[1], cross.at[1], d_send.at[1], d_recv.at[1], far).wait_recv()
            total = cross[0].astype(jnp.float32) + cross[1].astype(jnp.float32)
            outer[mine] = (total / 4.0).astype(jnp.bfloat16)
            start(outer.at[mine], outer.at[mine], d_send.at[2], d_recv.at[2], sibling)

    def update():
        with jax.named_scope("update"):
            copy(outer.at[1 - mine], outer.at[1 - mine], d_send.at[2], d_recv.at[2], sibling).wait_recv()
            loads[2].wait()
            for h in range(2):

                def one(g, _, h=h):
                    here = pl.ds(pl.multiple_of(g * LANES, LANES), LANES)
                    full = pl.ds(pl.multiple_of(h * n.half + g * LANES, LANES), LANES)
                    strided = pl.ds(h * n.groups + g, n.layers, stride=2 * n.groups)
                    grad = outer[h, 0 : n.layers, here].astype(jnp.float32)
                    moved = 0.9 * mom[strided, :] + grad
                    mom_out[strided, :] = moved
                    new_base = (base[:, full].astype(jnp.float32) - 0.7 * (grad + 0.9 * moved)).astype(jnp.bfloat16)
                    base_out[:, full] = new_base
                    local_out[:, full] = (
                        0.5 * loc[:, full].astype(jnp.float32) + 0.5 * new_base.astype(jnp.float32)
                    ).astype(jnp.bfloat16)
                    return 0

                lax.fori_loop(0, n.groups, one, 0)

    steps = (n.y // 2, n.x // 2)
    for s in range(1, max(steps)):
        with jax.named_scope("ring_step"):
            for c in range(n.chunks):
                for part in range(2):
                    if s < steps[part]:
                        for way in range(2):
                            arrived(part, c, way, s)
                            go(part, c, way, s + 1)
        if s == 1:
            average()
        if s == 2:
            update()
    if max(steps) < 2:
        average()
    if max(steps) < 3:
        update()

    loads[3].wait()
    totals = [jnp.zeros((n.tokens, n.rows), jnp.float32) for _ in range(2)]
    for c in range(n.chunks):
        for part in range(2):
            with jax.named_scope("last_wait"):
                for way in range(2):
                    arrived(part, c, way, steps[part])
            with jax.named_scope("matmul"):
                ring = rings[part][0]
                at_column = part * n.half + c * n.cols
                totals[part] += lax.dot_general(
                    tok[:, at_column : at_column + n.cols],
                    ring[c].reshape(n.rows, n.cols),
                    NT,
                    preferred_element_type=jnp.float32,
                )
    held = lax.broadcasted_iota(jnp.int32, (n.rows, n.rows), 0)
    wanted = lax.broadcasted_iota(jnp.int32, (n.rows, n.rows), 1)
    y_, x_, z_ = held // (n.x * n.z), (held // n.z) % n.x, held % n.z
    order = jnp.where((x_ * n.y + y_) * n.z + z_ == wanted, 1.0, 0.0)
    turned = jnp.dot(totals[0], order, precision=lax.Precision.HIGHEST, preferred_element_type=jnp.float32)
    proj_out[...] = ((turned + totals[1]) * (1.0 / math.sqrt(n.width))).astype(jnp.bfloat16)
    for c in sent:
        c.wait_send()


def build(n, tokens, local, base, momentum):
    bf16, f32 = jnp.bfloat16, jnp.float32
    most = max(n.x, n.y)
    dma = pltpu.SemaphoreType.DMA
    padded = -(-n.layers // 16) * 16
    return pl.pallas_call(
        functools.partial(kernel, n),
        out_shape=(
            jax.ShapeDtypeStruct((n.tokens, n.rows), bf16),
            jax.ShapeDtypeStruct((n.layers, n.width), bf16),
            jax.ShapeDtypeStruct((n.layers * n.width // LANES, LANES), f32),
            jax.ShapeDtypeStruct((n.layers, n.width), bf16),
        ),
        in_specs=[pl.BlockSpec(memory_space=pl.ANY)] * 4,
        out_specs=(pl.BlockSpec(memory_space=pltpu.VMEM),) * 4,
        scratch_shapes=[
            pltpu.VMEM((n.tokens, n.width), bf16),
            pltpu.VMEM((n.layers, n.width), bf16),
            pltpu.VMEM((n.layers, n.width), bf16),
            pltpu.VMEM((n.layers * n.width // LANES, LANES), f32),
            pltpu.VMEM((n.width // LANES, LANES), f32),
            pltpu.VMEM((2, n.z, n.groups, LANES), bf16),
            pltpu.VMEM((2, most, n.z, n.groups, LANES), bf16),
            pltpu.VMEM((most * n.z * n.groups, LANES), f32),
            pltpu.VMEM((n.chunks, n.y, n.x * n.z, n.cols), bf16),
            pltpu.VMEM((n.chunks, n.x, n.y * n.z, n.cols), bf16),
            pltpu.VMEM((2, padded, n.half), bf16),
            pltpu.VMEM((padded, n.half), bf16),
            pltpu.VMEM((2, padded, n.half), bf16),
            pltpu.VMEM((2, padded, n.half), bf16),
            dma((4,)),
            dma((n.z,)),
            dma((n.z,)),
            dma((2, most)),
            dma((2, most)),
            dma((2, n.chunks, 2, most // 2)),
            dma((2, n.chunks, 2, most // 2)),
            dma((3,)),
            dma((3,)),
        ],
        compiler_params=pltpu.CompilerParams(
            collective_id=0, has_side_effects=True, vmem_limit_bytes=40 * 1024 * 1024
        ),
    )(tokens, local, base, momentum)


def on_device(n, tokens, local_weights, base_weights, momentum):
    projected, new_base, new_momentum, new_local = build(
        n,
        tokens.reshape(n.tokens, n.width),
        local_weights.reshape(n.layers, n.width),
        base_weights.reshape(n.layers, n.width),
        momentum.reshape(n.layers * n.width // LANES, LANES),
    )
    return (
        projected[None],
        new_base.reshape(base_weights.shape),
        new_momentum.reshape(momentum.shape),
        new_local.reshape(local_weights.shape),
    )


def solution(mesh, n=Sizes(8, 8, 4, 8192, 10, 128, 4)):
    return jax.shard_map(
        functools.partial(on_device, n),
        mesh=mesh,
        in_specs=(
            P("rep", "fsdp", None),
            P("rep", None, "fsdp", None),
            P(None, "fsdp", None),
            P(None, "fsdp", None),
        ),
        out_specs=(
            P("rep", "fsdp", None),
            P(None, "fsdp", None),
            P(None, "fsdp", None),
            P("rep", None, "fsdp", None),
        ),
        check_vma=False,
    )
```

```python
import functools
import math

import jax
import jax.numpy as jnp
from jax import lax
from jax.experimental import pallas as pl
from jax.experimental.pallas import tpu as pltpu
from jax.sharding import PartitionSpec as P

LANES = 128
MIB = 1024 * 1024
FIRST = {2: (1,), 4: (2, 1), 8: (2, 1)}
MESH = pl.DeviceIdType.MESH
NT = (((1,), (1,)), ((), ()))


class Sizes:
    def __init__(self, x, y, z, width, layers, tokens, chunks, batches=1):
        self.x, self.y, self.z = x, y, z
        self.width, self.layers, self.tokens = width, layers, tokens
        self.chunks, self.batches = chunks, batches
        self.rows = x * y * z
        self.half = width // 2
        self.part = width // 4
        self.cols = self.part // chunks
        self.groups = self.part // LANES
        self.lanes = width // LANES


def kernel(
    n,
    tok_hbm, loc_hbm, base_hbm, mom_hbm,
    proj_out, base_out, mom_out, local_out,
    tok, stage, loc, base, mom, dense, row, code, zbuf, plane, wide, ring_a, ring_b, order, give, take,
    delta, pair, cross, outer,
    load_sem, far_in, t_send, t_recv, z_send, z_recv, p_send, p_recv, r_send, r_recv, d_send, d_recv, g_send, g_recv,
):
    bf16, f32 = jnp.bfloat16, jnp.float32
    rep, me = lax.axis_index("rep"), lax.axis_index("fsdp")
    x, y, z = me // (n.y * n.z), (me // n.z) % n.y, me % n.z
    side = z % 2
    late = rep // 2
    mine = rep % 2

    def at(x_, y_, z_):
        return {"fsdp": (x_ * n.y + y_) * n.z + z_}

    sibling = {"rep": rep + 1 - 2 * mine}
    far = {"rep": lax.rem(rep + 2, 4)}
    partner = at(x, y, z + 1 - 2 * side)

    def x_peer(k):
        return at(lax.rem(x + k, n.x), y, z)

    def y_peer(k):
        return at(x, lax.rem(y + k, n.y), z)

    def z_peer(k):
        return at(x, y, lax.rem(z + k, n.z))

    loads = [
        pltpu.make_async_copy(src, dst, load_sem.at[i])
        for i, (src, dst) in enumerate(
            (
                (loc_hbm, loc),
                (base_hbm, base),
                (mom_hbm, mom),
            )
        )
    ]
    for i in range(2 * n.chunks):
        for own in range(2):
            from_ = (1 - side if own == 0 else side) * n.half + i * n.cols
            loads.append(
                pltpu.make_async_copy(
                    tok_hbm.at[:, pl.ds(pl.multiple_of(from_, n.cols), n.cols)],
                    stage.at[i] if own == 0 else tok.at[i, 0 : n.tokens],
                    load_sem.at[3 + 2 * i + own],
                )
            )
    loads[0].start()

    barrier = pltpu.get_barrier_semaphore()
    peers = (
        [sibling]
        + [z_peer(k) for k in range(1, n.z)]
        + [x_peer(k) for k in range(1, n.x)]
        + [y_peer(k) for k in range(1, n.y)]
    )
    for peer in peers:
        pl.semaphore_signal(barrier, inc=1, device_id=peer, device_id_type=MESH)

    @pl.when(late == 0)
    def _():
        pl.semaphore_signal(barrier, inc=1, device_id=far, device_id_type=MESH)

    for load in loads[1:]:
        load.start()

    def copy(src, dst, send, recv, peer):
        return pltpu.make_async_remote_copy(
            src_ref=src, dst_ref=dst, send_sem=send, recv_sem=recv, device_id=peer, device_id_type=MESH
        )

    sent = []

    def start(src, dst, send, recv, peer, listed=True):
        c = copy(src, dst, send, recv, peer)
        c.start()
        if listed:
            sent.append(c)

    def flush(left=0):
        while len(sent) > left:
            sent.pop(0).wait_send()

    loads[0].wait()
    first = loc[0:1, :].astype(f32)
    for g in range(n.lanes):
        row[g : g + 1, :] = first[:, g * LANES : (g + 1) * LANES]
    code[...] = row[...].astype(bf16).reshape(code.shape)
    zbuf[:, z] = code[side]

    pl.semaphore_wait(barrier, len(peers) + late)

    @pl.when(late == 1)
    def _():
        pl.semaphore_signal(far_in, inc=1, device_id=far, device_id_type=MESH)

    for k in range(1, n.z):
        start(code.at[lax.rem(z + k, 2)], zbuf.at[:, z], z_send.at[k], z_recv.at[k], z_peer(k))

    loads[1].wait()
    packed = n.layers * 2 * n.groups

    def lane_groups():
        for h in range(2):
            for g in range(2 * n.groups):
                at_lane = h * n.half + g * LANES
                yield slice(at_lane, at_lane + LANES), pl.ds(h * packed + g, n.layers, stride=2 * n.groups), h, g

    for here, spread, _, _ in lane_groups():
        dense[spread, :] = base[:, here].astype(f32) - loc[:, here].astype(f32)
    delta[...] = dense[...].astype(bf16).reshape(delta.shape)

    start(delta.at[1 - mine], pair, d_send.at[0], d_recv.at[0], sibling)

    def token_copy(i):
        there = tok.at[i, n.tokens : 2 * n.tokens]
        return copy(stage.at[i], there, t_send.at[i], t_recv.at[i], partner)

    token_copies = [token_copy(i) for i in range(2 * n.chunks)]
    for i in range(2 * n.chunks):
        loads[3 + 2 * i].wait()

    def send_tokens():
        for c in token_copies:
            c.start()

    pl.when(late == 0)(send_tokens)

    held = lax.broadcasted_iota(jnp.int32, (n.rows, 1), 0)
    xb, yb, zb = (size.bit_length() - 1 for size in (n.x, n.y, n.z))
    wanted = (((held >> zb) & (n.x - 1)) << (yb + zb)) | ((held >> (xb + zb)) << zb) | (held & (n.z - 1))
    spot = lax.broadcasted_iota(jnp.int32, (n.rows, n.rows), 1)
    order[...] = jnp.where(wanted == spot, 1.0, 0.0).astype(bf16)

    copy(pair, pair, d_send.at[0], d_recv.at[0], sibling).wait_recv()
    cross[0] = (delta[mine].astype(f32) + pair[...].astype(f32)).astype(bf16)

    far_copy = copy(cross.at[0], cross.at[1], d_send.at[1], d_recv.at[1], far)

    @pl.when(late == 1)
    def _():
        far_copy.start()
        send_tokens()

    for b in range(n.batches):
        deep = slice(b * n.z // n.batches, (b + 1) * n.z // n.batches)
        for slot in range(deep.start, deep.stop):

            @pl.when(z != slot)
            def _():
                k = lax.rem(z - slot + n.z, n.z)
                copy(zbuf.at[:, slot], zbuf.at[:, slot], z_send.at[k], z_recv.at[k], sibling).wait_recv()

        for k in range(1, max(n.x, n.y)):
            if k < n.x:
                start(zbuf.at[0, deep], plane.at[0, x, deep], p_send.at[0], p_recv.at[0], x_peer(k), False)
            if k < n.y:
                start(zbuf.at[1, deep], plane.at[1, y, deep], p_send.at[1], p_recv.at[1], y_peer(k), False)
    rings = ((ring_a, y, n.y, y_peer, x, n.x), (ring_b, x, n.x, x_peer, y, n.y))

    def block_rows(part):
        return rings[part][5] * n.z

    def hop(part, c, way, distance, length, inward):
        ring, p, size, peer, _, _ = rings[part]
        rows = block_rows(part)
        away = distance if inward else distance - length
        block = lax.rem(p + (size - away if way == 0 else away), size)
        cut = pl.ds(0, rows)
        if distance == size // 2:
            cut = pl.ds(0, rows // 2) if way == 0 else pl.ds(rows // 2, rows // 2)
        sems = (r_send.at[part, c, way, distance - 1], r_recv.at[part, c, way, distance - 1])
        slot = ring.at[c, block, cut]
        return copy(slot, slot, *sems, peer(length if way == 0 else size - length))

    def go(part, c, way, distance, length):
        sent.append(hop(part, c, way, distance, length, False))
        sent[-1].start()

    def arrived(part, c, way, distance):
        hop(part, c, way, distance, 1, True).wait_recv()

    for part in range(2):
        ring, p, _, _, other, count = rings[part]
        others = plane.at[part, 0 : count - 1]
        gathered = copy(others, others, p_send.at[part], p_recv.at[part], sibling)
        gathered.wait_recv()
        sent.append(gathered)
        plane[part, other] = zbuf[part]
        rows = block_rows(part)
        wide[0 : rows * n.groups, :] = plane[part, 0:count].reshape(rows * n.groups, LANES).astype(f32)
        per = n.cols // LANES
        for c in range(n.chunks):
            for i in range(per):
                ring[c, p, :, i * LANES : (i + 1) * LANES] = wide[
                    pl.ds(c * per + i, rows, stride=n.groups), :
                ].astype(bf16)
            for distance in FIRST[rings[part][2]]:
                for way in range(2):
                    go(part, c, way, distance, distance)

    @pl.when(late == 0)
    def _():
        pl.semaphore_wait(far_in, 1)
        far_copy.start()

    sent.append(far_copy)

    outer_copy = copy(outer.at[mine], outer.at[mine], d_send.at[2], d_recv.at[2], sibling)

    def average():
        copy(cross.at[1], cross.at[1], d_send.at[1], d_recv.at[1], far).wait_recv()
        outer[mine] = ((cross[0].astype(f32) + cross[1].astype(f32)) / 4.0).astype(bf16)
        outer_copy.start()

    for c in range(n.chunks):
        for part in range(2):
            if rings[part][2] == 8:
                for way in range(2):
                    arrived(part, c, way, 2)
                    go(part, c, way, 3, 1)
                    go(part, c, way, 4, 2)
    pl.when(late == 1)(average)

    for i in range(2 * n.chunks):
        loads[4 + 2 * i].wait()

    def product(part, c):
        size = rings[part][2]
        for distance in range(1, size // 2 + 1):
            if not (size == 8 and distance == 2):
                for way in range(2):
                    arrived(part, c, way, distance)
        i = part * n.chunks + c
        token_copy(i).wait_recv()
        return lax.dot_general(
            tok[i],
            rings[part][0][c].reshape(n.rows, n.cols),
            NT,
            preferred_element_type=f32,
        )

    def turn(a):
        high = a.astype(bf16)
        low = (a - high.astype(f32)).astype(bf16)
        return sum(jnp.dot(half, order[...], preferred_element_type=f32) for half in (high, low))

    first_sum = product(0, 0)
    for c in range(1, n.chunks):
        first_sum += product(0, c)
    total = turn(first_sum)
    for c in range(n.chunks):
        total += product(1, c)
    give[...] = total[n.tokens :].astype(bf16)
    start(give, take, g_send, g_recv, partner)
    pl.when(late == 0)(average)
    flush(1)
    sent.append(outer_copy)

    copy(give, take, g_send, g_recv, partner).wait_recv()
    proj_out[...] = ((total[: n.tokens] + take[...].astype(f32)) * (1.0 / math.sqrt(n.width))).astype(bf16)
    copy(outer.at[1 - mine], outer.at[1 - mine], d_send.at[2], d_recv.at[2], sibling).wait_recv()
    loads[2].wait()
    dense[...] = outer[...].reshape(dense.shape).astype(f32)
    for here, spread, h, g in lane_groups():
        strided = pl.ds(h * 2 * n.groups + g, n.layers, stride=n.lanes)
        grad = dense[spread, :]
        moved = 0.9 * mom[strided, :] + grad
        mom_out[strided, :] = moved
        new_base = (base[:, here].astype(f32) - 0.7 * (grad + 0.9 * moved)).astype(bf16)
        base_out[:, here] = new_base
        local_out[:, here] = (0.5 * loc[:, here].astype(f32) + 0.5 * new_base.astype(f32)).astype(bf16)

    flush()
    for c in token_copies:
        c.wait_send()


def build(n, tokens, local, base, momentum):
    bf16, f32 = jnp.bfloat16, jnp.float32
    most = max(n.x, n.y)
    dma = pltpu.SemaphoreType.DMA
    packed = n.layers * 2 * n.groups
    arrays = [pltpu.with_memory_space_constraint(a, pltpu.HBM) for a in (tokens, local, base, momentum)]
    return pl.pallas_call(
        functools.partial(kernel, n),
        out_shape=(
            pltpu.VMEM((n.tokens, n.rows), bf16),
            pltpu.VMEM((n.layers, n.width), bf16),
            pltpu.VMEM((n.layers * n.lanes, LANES), f32),
            pltpu.VMEM((n.layers, n.width), bf16),
        ),
        in_specs=[pl.BlockSpec(memory_space=pl.ANY)] * 4,
        out_specs=(pl.BlockSpec(memory_space=pltpu.VMEM),) * 4,
        scratch_shapes=[
            pltpu.VMEM((2 * n.chunks, 2 * n.tokens, n.cols), bf16),
            pltpu.VMEM((2 * n.chunks, n.tokens, n.cols), bf16),
            pltpu.VMEM((n.layers, n.width), bf16),
            pltpu.VMEM((n.layers, n.width), bf16),
            pltpu.VMEM((n.layers * n.lanes, LANES), f32),
            pltpu.VMEM((n.layers * n.lanes, LANES), f32),
            pltpu.VMEM((n.lanes, LANES), f32),
            pltpu.VMEM((2, 2, n.groups, LANES), bf16),
            pltpu.VMEM((2, n.z, n.groups, LANES), bf16),
            pltpu.VMEM((2, most, n.z, n.groups, LANES), bf16),
            pltpu.VMEM((most * n.z * n.groups, LANES), f32),
            pltpu.VMEM((n.chunks, n.y, n.x * n.z, n.cols), bf16),
            pltpu.VMEM((n.chunks, n.x, n.y * n.z, n.cols), bf16),
            pltpu.VMEM((n.rows, n.rows), bf16),
            pltpu.VMEM((n.tokens, n.rows), bf16),
            pltpu.VMEM((n.tokens, n.rows), bf16),
            pltpu.VMEM((2, packed, LANES), bf16),
            pltpu.VMEM((packed, LANES), bf16),
            pltpu.VMEM((2, packed, LANES), bf16),
            pltpu.VMEM((2, packed, LANES), bf16),
            dma((3 + 4 * n.chunks,)),
            pltpu.SemaphoreType.REGULAR,
            dma((2 * n.chunks,)),
            dma((2 * n.chunks,)),
            dma((n.z,)),
            dma((n.z,)),
            dma((2,)),
            dma((2,)),
            dma((2, n.chunks, 2, most // 2)),
            dma((2, n.chunks, 2, most // 2)),
            dma((3,)),
            dma((3,)),
            dma,
            dma,
        ],
        compiler_params=pltpu.CompilerParams(collective_id=0, has_side_effects=True, vmem_limit_bytes=40 * MIB),
    )(*arrays)


def store_kernel(*refs):
    copies = [pltpu.make_async_copy(refs[i], refs[4 + i], refs[8].at[i]) for i in range(4)]
    for one in copies:
        one.start()
    for one in copies:
        one.wait()


def store(*arrays):
    return pl.pallas_call(
        store_kernel,
        out_shape=tuple(jax.ShapeDtypeStruct(a.shape, a.dtype) for a in arrays),
        in_specs=[pl.BlockSpec(memory_space=pltpu.VMEM)] * 4,
        out_specs=(pl.BlockSpec(memory_space=pl.ANY),) * 4,
        scratch_shapes=[pltpu.SemaphoreType.DMA((4,))],
        compiler_params=pltpu.CompilerParams(vmem_limit_bytes=8 * MIB),
    )(*arrays)


def on_device(n, tokens, local_weights, base_weights, momentum):
    projected, new_base, new_momentum, new_local = store(
        *build(
            n,
            tokens.reshape(n.tokens, n.width),
            local_weights.reshape(n.layers, n.width),
            base_weights.reshape(n.layers, n.width),
            momentum.reshape(n.layers * n.lanes, LANES),
        )
    )
    return (
        projected[None],
        new_base.reshape(base_weights.shape),
        new_momentum.reshape(momentum.shape),
        new_local.reshape(local_weights.shape),
    )


def solution(mesh, n=Sizes(8, 8, 4, 8192, 10, 128, 2)):
    return jax.shard_map(
        functools.partial(on_device, n),
        mesh=mesh,
        in_specs=(
            P("rep", "fsdp", None),
            P("rep", None, "fsdp", None),
            P(None, "fsdp", None),
            P(None, "fsdp", None),
        ),
        out_specs=(
            P("rep", "fsdp", None),
            P(None, "fsdp", None),
            P(None, "fsdp", None),
            P("rep", None, "fsdp", None),
        ),
        check_vma=False,
    )
```

```python
import functools
import math

import jax
import jax.numpy as jnp
from jax import lax
from jax.experimental import pallas as pl
from jax.experimental.pallas import tpu as pltpu
from jax.sharding import PartitionSpec as P

LANES = 128
MIB = 1024 * 1024
FIRST = {2: (1,), 4: (2, 1), 8: (2, 1)}
MESH = pl.DeviceIdType.MESH
NT = (((1,), (1,)), ((), ()))


class Sizes:
    def __init__(self, x, y, z, width, layers, tokens, chunks, batches=1):
        self.x, self.y, self.z = x, y, z
        self.width, self.layers, self.tokens = width, layers, tokens
        self.chunks, self.batches = chunks, batches
        self.rows = x * y * z
        self.half = width // 2
        self.part = width // 4
        self.cols = self.part // chunks
        self.groups = self.part // LANES
        self.lanes = width // LANES


def kernel(
    n,
    tok_hbm, loc_hbm, base_hbm, mom_hbm,
    proj_out, base_out, mom_out, local_out,
    tok, stage, loc, base, mom, dense, row, code, zbuf, plane, wide, ring_a, ring_b, order, give, take,
    delta, pair, cross, outer,
    load_sem, far_in, t_send, t_recv, z_send, z_recv, p_send, p_recv, r_send, r_recv, d_send, d_recv, g_send, g_recv,
):
    bf16, f32 = jnp.bfloat16, jnp.float32
    rep, me = lax.axis_index("rep"), lax.axis_index("fsdp")
    x, y, z = me // (n.y * n.z), (me // n.z) % n.y, me % n.z
    side = z % 2
    late = rep // 2
    mine = rep % 2

    def at(x_, y_, z_):
        return {"fsdp": (x_ * n.y + y_) * n.z + z_}

    sibling = {"rep": rep + 1 - 2 * mine}
    far = {"rep": lax.rem(rep + 2, 4)}
    partner = at(x, y, z + 1 - 2 * side)

    def x_peer(k):
        return at(lax.rem(x + k, n.x), y, z)

    def y_peer(k):
        return at(x, lax.rem(y + k, n.y), z)

    def z_peer(k):
        return at(x, y, lax.rem(z + k, n.z))

    loads = [
        pltpu.make_async_copy(src, dst, load_sem.at[i])
        for i, (src, dst) in enumerate(
            (
                (loc_hbm, loc),
                (base_hbm, base),
                (mom_hbm, mom),
            )
        )
    ]
    for i in range(2 * n.chunks):
        for own in range(2):
            from_ = (1 - side if own == 0 else side) * n.half + i * n.cols
            loads.append(
                pltpu.make_async_copy(
                    tok_hbm.at[:, pl.ds(pl.multiple_of(from_, n.cols), n.cols)],
                    stage.at[i] if own == 0 else tok.at[i, 0 : n.tokens],
                    load_sem.at[3 + 2 * i + own],
                )
            )
    loads[0].start()

    barrier = pltpu.get_barrier_semaphore()
    peers = (
        [sibling]
        + [z_peer(k) for k in range(1, n.z)]
        + [x_peer(k) for k in range(1, n.x)]
        + [y_peer(k) for k in range(1, n.y)]
    )
    for peer in peers:
        pl.semaphore_signal(barrier, inc=1, device_id=peer, device_id_type=MESH)

    @pl.when(late == 0)
    def _():
        pl.semaphore_signal(barrier, inc=1, device_id=far, device_id_type=MESH)

    for load in loads[1:]:
        load.start()

    def copy(src, dst, send, recv, peer):
        return pltpu.make_async_remote_copy(
            src_ref=src, dst_ref=dst, send_sem=send, recv_sem=recv, device_id=peer, device_id_type=MESH
        )

    sent = []

    def start(src, dst, send, recv, peer, listed=True):
        c = copy(src, dst, send, recv, peer)
        c.start()
        if listed:
            sent.append(c)

    def flush(left=0):
        while len(sent) > left:
            sent.pop(0).wait_send()

    loads[0].wait()
    first = loc[0:1, :].astype(f32)
    for g in range(n.lanes):
        row[g : g + 1, :] = first[:, g * LANES : (g + 1) * LANES]
    code[...] = row[...].astype(bf16).reshape(code.shape)
    zbuf[:, z] = code[side]

    pl.semaphore_wait(barrier, len(peers) + late)

    @pl.when(late == 1)
    def _():
        pl.semaphore_signal(far_in, inc=1, device_id=far, device_id_type=MESH)

    for k in range(1, n.z):
        start(code.at[lax.rem(z + k, 2)], zbuf.at[:, z], z_send.at[k], z_recv.at[k], z_peer(k))

    loads[1].wait()
    packed = n.layers * 2 * n.groups

    def lane_groups():
        for h in range(2):
            for g in range(2 * n.groups):
                at_lane = h * n.half + g * LANES
                yield slice(at_lane, at_lane + LANES), pl.ds(h * packed + g, n.layers, stride=2 * n.groups), h, g

    for here, spread, _, _ in lane_groups():
        dense[spread, :] = base[:, here].astype(f32) - loc[:, here].astype(f32)
    delta[...] = dense[...].astype(bf16).reshape(delta.shape)

    start(delta.at[1 - mine], pair, d_send.at[0], d_recv.at[0], sibling)

    def token_copy(i):
        there = tok.at[i, n.tokens : 2 * n.tokens]
        return copy(stage.at[i], there, t_send.at[i], t_recv.at[i], partner)

    token_copies = [token_copy(i) for i in range(2 * n.chunks)]
    for i in range(2 * n.chunks):
        loads[3 + 2 * i].wait()

    def send_tokens():
        for c in token_copies:
            c.start()

    pl.when(late == 0)(send_tokens)

    held = lax.broadcasted_iota(jnp.int32, (n.rows, 1), 0)
    xb, yb, zb = (size.bit_length() - 1 for size in (n.x, n.y, n.z))
    wanted = (((held >> zb) & (n.x - 1)) << (yb + zb)) | ((held >> (xb + zb)) << zb) | (held & (n.z - 1))
    spot = lax.broadcasted_iota(jnp.int32, (n.rows, n.rows), 1)
    order[...] = jnp.where(wanted == spot, 1.0, 0.0).astype(bf16)

    copy(pair, pair, d_send.at[0], d_recv.at[0], sibling).wait_recv()
    cross[0] = (delta[mine].astype(f32) + pair[...].astype(f32)).astype(bf16)

    far_copy = copy(cross.at[0], cross.at[1], d_send.at[1], d_recv.at[1], far)

    @pl.when(late == 1)
    def _():
        far_copy.start()
        send_tokens()

    for b in range(n.batches):
        deep = slice(b * n.z // n.batches, (b + 1) * n.z // n.batches)
        for slot in range(deep.start, deep.stop):

            @pl.when(z != slot)
            def _():
                k = lax.rem(z - slot + n.z, n.z)
                copy(zbuf.at[:, slot], zbuf.at[:, slot], z_send.at[k], z_recv.at[k], sibling).wait_recv()

        for k in sorted(range(1, max(n.x, n.y)), key=lambda k: -min(k, max(n.x, n.y) - k)):
            if k < n.x:
                start(zbuf.at[0, deep], plane.at[0, x, deep], p_send.at[0], p_recv.at[0], x_peer(k), False)
            if k < n.y:
                start(zbuf.at[1, deep], plane.at[1, y, deep], p_send.at[1], p_recv.at[1], y_peer(k), False)
    rings = ((ring_a, y, n.y, y_peer, x, n.x), (ring_b, x, n.x, x_peer, y, n.y))

    def block_rows(part):
        return rings[part][5] * n.z

    def hop(part, c, way, distance, length, inward):
        ring, p, size, peer, _, _ = rings[part]
        rows = block_rows(part)
        away = distance if inward else distance - length
        block = lax.rem(p + (size - away if way == 0 else away), size)
        cut = pl.ds(0, rows)
        if distance == size // 2:
            cut = pl.ds(0, rows // 2) if way == 0 else pl.ds(rows // 2, rows // 2)
        sems = (r_send.at[part, c, way, distance - 1], r_recv.at[part, c, way, distance - 1])
        slot = ring.at[c, block, cut]
        return copy(slot, slot, *sems, peer(length if way == 0 else size - length))

    def go(part, c, way, distance, length):
        sent.append(hop(part, c, way, distance, length, False))
        sent[-1].start()

    def arrived(part, c, way, distance):
        hop(part, c, way, distance, 1, True).wait_recv()

    for part in range(2):
        ring, p, _, _, other, count = rings[part]
        others = plane.at[part, 0 : count - 1]
        gathered = copy(others, others, p_send.at[part], p_recv.at[part], sibling)
        gathered.wait_recv()
        sent.append(gathered)
        plane[part, other] = zbuf[part]
        rows = block_rows(part)
        wide[0 : rows * n.groups, :] = plane[part, 0:count].reshape(rows * n.groups, LANES).astype(f32)
        per = n.cols // LANES
        for c in range(n.chunks):
            for i in range(per):
                ring[c, p, :, i * LANES : (i + 1) * LANES] = wide[
                    pl.ds(c * per + i, rows, stride=n.groups), :
                ].astype(bf16)
            for distance in FIRST[rings[part][2]]:
                for way in range(2):
                    go(part, c, way, distance, distance)

    @pl.when(late == 0)
    def _():
        pl.semaphore_wait(far_in, 1)
        far_copy.start()

    sent.append(far_copy)

    outer_copy = copy(outer.at[mine], outer.at[mine], d_send.at[2], d_recv.at[2], sibling)

    def average():
        copy(cross.at[1], cross.at[1], d_send.at[1], d_recv.at[1], far).wait_recv()
        outer[mine] = ((cross[0].astype(f32) + cross[1].astype(f32)) / 4.0).astype(bf16)
        outer_copy.start()

    for c in range(n.chunks):
        for part in range(2):
            if rings[part][2] == 8:
                for way in range(2):
                    arrived(part, c, way, 2)
                    go(part, c, way, 3, 1)
                    go(part, c, way, 4, 2)
    average()
    sent.append(outer_copy)
    copy(outer.at[1 - mine], outer.at[1 - mine], d_send.at[2], d_recv.at[2], sibling).wait_recv()
    loads[2].wait()
    dense[...] = outer[...].reshape(dense.shape).astype(f32)
    for here, spread, h, g in lane_groups():
        strided = pl.ds(h * 2 * n.groups + g, n.layers, stride=n.lanes)
        grad = dense[spread, :]
        moved = 0.9 * mom[strided, :] + grad
        mom_out[strided, :] = moved
        new_base = (base[:, here].astype(f32) - 0.7 * (grad + 0.9 * moved)).astype(bf16)
        base_out[:, here] = new_base
        local_out[:, here] = (0.5 * loc[:, here].astype(f32) + 0.5 * new_base.astype(f32)).astype(bf16)

    for i in range(2 * n.chunks):
        loads[4 + 2 * i].wait()

    def product(part, c):
        size = rings[part][2]
        for distance in range(1, size // 2 + 1):
            if not (size == 8 and distance == 2):
                for way in range(2):
                    arrived(part, c, way, distance)
        i = part * n.chunks + c
        token_copy(i).wait_recv()
        return lax.dot_general(
            tok[i],
            rings[part][0][c].reshape(n.rows, n.cols),
            NT,
            preferred_element_type=f32,
        )

    def turn(a):
        high = a.astype(bf16)
        low = (a - high.astype(f32)).astype(bf16)
        return sum(jnp.dot(half, order[...], preferred_element_type=f32) for half in (high, low))

    first_sum = product(0, 0)
    for c in range(1, n.chunks):
        first_sum += product(0, c)
    total = turn(first_sum)
    for c in range(n.chunks):
        total += product(1, c)
    give[...] = total[n.tokens :].astype(bf16)
    start(give, take, g_send, g_recv, partner)
    flush(1)

    copy(give, take, g_send, g_recv, partner).wait_recv()
    proj_out[...] = ((total[: n.tokens] + take[...].astype(f32)) * (1.0 / math.sqrt(n.width))).astype(bf16)
    flush()
    for c in token_copies:
        c.wait_send()


def build(n, tokens, local, base, momentum):
    bf16, f32 = jnp.bfloat16, jnp.float32
    most = max(n.x, n.y)
    dma = pltpu.SemaphoreType.DMA
    packed = n.layers * 2 * n.groups
    arrays = [pltpu.with_memory_space_constraint(a, pltpu.HBM) for a in (tokens, local, base, momentum)]
    return pl.pallas_call(
        functools.partial(kernel, n),
        out_shape=(
            pltpu.VMEM((n.tokens, n.rows), bf16),
            pltpu.VMEM((n.layers, n.width), bf16),
            pltpu.VMEM((n.layers * n.lanes, LANES), f32),
            pltpu.VMEM((n.layers, n.width), bf16),
        ),
        in_specs=[pl.BlockSpec(memory_space=pl.ANY)] * 4,
        out_specs=(pl.BlockSpec(memory_space=pltpu.VMEM),) * 4,
        scratch_shapes=[
            pltpu.VMEM((2 * n.chunks, 2 * n.tokens, n.cols), bf16),
            pltpu.VMEM((2 * n.chunks, n.tokens, n.cols), bf16),
            pltpu.VMEM((n.layers, n.width), bf16),
            pltpu.VMEM((n.layers, n.width), bf16),
            pltpu.VMEM((n.layers * n.lanes, LANES), f32),
            pltpu.VMEM((n.layers * n.lanes, LANES), f32),
            pltpu.VMEM((n.lanes, LANES), f32),
            pltpu.VMEM((2, 2, n.groups, LANES), bf16),
            pltpu.VMEM((2, n.z, n.groups, LANES), bf16),
            pltpu.VMEM((2, most, n.z, n.groups, LANES), bf16),
            pltpu.VMEM((most * n.z * n.groups, LANES), f32),
            pltpu.VMEM((n.chunks, n.y, n.x * n.z, n.cols), bf16),
            pltpu.VMEM((n.chunks, n.x, n.y * n.z, n.cols), bf16),
            pltpu.VMEM((n.rows, n.rows), bf16),
            pltpu.VMEM((n.tokens, n.rows), bf16),
            pltpu.VMEM((n.tokens, n.rows), bf16),
            pltpu.VMEM((2, packed, LANES), bf16),
            pltpu.VMEM((packed, LANES), bf16),
            pltpu.VMEM((2, packed, LANES), bf16),
            pltpu.VMEM((2, packed, LANES), bf16),
            dma((3 + 4 * n.chunks,)),
            pltpu.SemaphoreType.REGULAR,
            dma((2 * n.chunks,)),
            dma((2 * n.chunks,)),
            dma((n.z,)),
            dma((n.z,)),
            dma((2,)),
            dma((2,)),
            dma((2, n.chunks, 2, most // 2)),
            dma((2, n.chunks, 2, most // 2)),
            dma((3,)),
            dma((3,)),
            dma,
            dma,
        ],
        compiler_params=pltpu.CompilerParams(collective_id=0, has_side_effects=True, vmem_limit_bytes=40 * MIB),
    )(*arrays)


def store_kernel(*refs):
    copies = [pltpu.make_async_copy(refs[i], refs[4 + i], refs[8].at[i]) for i in range(4)]
    for one in copies:
        one.start()
    for one in copies:
        one.wait()


def store(*arrays):
    return pl.pallas_call(
        store_kernel,
        out_shape=tuple(jax.ShapeDtypeStruct(a.shape, a.dtype) for a in arrays),
        in_specs=[pl.BlockSpec(memory_space=pltpu.VMEM)] * 4,
        out_specs=(pl.BlockSpec(memory_space=pl.ANY),) * 4,
        scratch_shapes=[pltpu.SemaphoreType.DMA((4,))],
        compiler_params=pltpu.CompilerParams(vmem_limit_bytes=8 * MIB),
    )(*arrays)


def on_device(n, tokens, local_weights, base_weights, momentum):
    projected, new_base, new_momentum, new_local = store(
        *build(
            n,
            tokens.reshape(n.tokens, n.width),
            local_weights.reshape(n.layers, n.width),
            base_weights.reshape(n.layers, n.width),
            momentum.reshape(n.layers * n.lanes, LANES),
        )
    )
    return (
        projected[None],
        new_base.reshape(base_weights.shape),
        new_momentum.reshape(momentum.shape),
        new_local.reshape(local_weights.shape),
    )


def solution(mesh, n=Sizes(8, 8, 4, 8192, 10, 128, 1)):
    return jax.shard_map(
        functools.partial(on_device, n),
        mesh=mesh,
        in_specs=(
            P("rep", "fsdp", None),
            P("rep", None, "fsdp", None),
            P(None, "fsdp", None),
            P(None, "fsdp", None),
        ),
        out_specs=(
            P("rep", "fsdp", None),
            P(None, "fsdp", None),
            P(None, "fsdp", None),
            P("rep", None, "fsdp", None),
        ),
        check_vma=False,
    )
```

```python
import functools
import math

import jax
import jax.numpy as jnp
from jax import lax
from jax.experimental import pallas as pl
from jax.experimental.pallas import tpu as pltpu
from jax.sharding import PartitionSpec as P

LANES = 128
MIB = 1024 * 1024
FIRST = {2: (1,), 4: (2, 1), 8: (2, 1)}
MESH = pl.DeviceIdType.MESH
NT = (((1,), (1,)), ((), ()))


class Sizes:
    def __init__(self, x, y, z, width, layers, tokens, chunks, batches=1):
        self.x, self.y, self.z = x, y, z
        self.width, self.layers, self.tokens = width, layers, tokens
        self.chunks, self.batches = chunks, batches
        self.rows = x * y * z
        self.half = width // 2
        self.part = width // 4
        self.cols = self.part // chunks
        self.groups = self.part // LANES
        self.lanes = width // LANES


def kernel(
    n,
    tok_hbm, loc_hbm, base_hbm, mom_hbm,
    proj_out, base_out, mom_out, local_out,
    tok, stage, loc, base, mom, dense, row, code, zbuf, plane, wide, ring_a, ring_b, order, give, take,
    delta, pair, cross, outer,
    load_sem, far_in, t_send, t_recv, z_send, z_recv, p_send, p_recv, r_send, r_recv, d_send, d_recv, g_send, g_recv,
):
    bf16, f32 = jnp.bfloat16, jnp.float32
    rep, me = lax.axis_index("rep"), lax.axis_index("fsdp")
    x, y, z = me // (n.y * n.z), (me // n.z) % n.y, me % n.z
    side = z % 2
    late = rep // 2
    mine = rep % 2

    def at(x_, y_, z_):
        return {"fsdp": (x_ * n.y + y_) * n.z + z_}

    sibling = {"rep": rep + 1 - 2 * mine}
    far = {"rep": lax.rem(rep + 2, 4)}
    partner = at(x, y, z + 1 - 2 * side)

    def x_peer(k):
        return at(lax.rem(x + k, n.x), y, z)

    def y_peer(k):
        return at(x, lax.rem(y + k, n.y), z)

    def z_peer(k):
        return at(x, y, lax.rem(z + k, n.z))

    loads = [
        pltpu.make_async_copy(src, dst, load_sem.at[i])
        for i, (src, dst) in enumerate(
            (
                (loc_hbm, loc),
                (base_hbm, base),
                (mom_hbm, mom),
            )
        )
    ]
    for i in range(2 * n.chunks):
        for own in range(2):
            from_ = (1 - side if own == 0 else side) * n.half + i * n.cols
            loads.append(
                pltpu.make_async_copy(
                    tok_hbm.at[:, pl.ds(pl.multiple_of(from_, n.cols), n.cols)],
                    stage.at[i] if own == 0 else tok.at[i, 0 : n.tokens],
                    load_sem.at[3 + 2 * i + own],
                )
            )
    loads[0].start()

    barrier = pltpu.get_barrier_semaphore()
    peers = (
        [sibling]
        + [z_peer(k) for k in range(1, n.z)]
        + [x_peer(k) for k in range(1, n.x)]
        + [y_peer(k) for k in range(1, n.y)]
    )
    for peer in peers:
        pl.semaphore_signal(barrier, inc=1, device_id=peer, device_id_type=MESH)

    @pl.when(late == 0)
    def _():
        pl.semaphore_signal(barrier, inc=1, device_id=far, device_id_type=MESH)

    for load in loads[1:]:
        load.start()

    def copy(src, dst, send, recv, peer):
        return pltpu.make_async_remote_copy(
            src_ref=src, dst_ref=dst, send_sem=send, recv_sem=recv, device_id=peer, device_id_type=MESH
        )

    sent = []

    def start(src, dst, send, recv, peer, listed=True):
        c = copy(src, dst, send, recv, peer)
        c.start()
        if listed:
            sent.append(c)

    def flush(left=0):
        while len(sent) > left:
            sent.pop(0).wait_send()

    loads[0].wait()
    first = loc[0:1, :].astype(f32)
    for g in range(n.lanes):
        row[g : g + 1, :] = first[:, g * LANES : (g + 1) * LANES]
    code[...] = row[...].astype(bf16).reshape(code.shape)
    zbuf[:, z] = code[side]

    pl.semaphore_wait(barrier, len(peers) + late)

    @pl.when(late == 1)
    def _():
        pl.semaphore_signal(far_in, inc=1, device_id=far, device_id_type=MESH)

    for k in range(1, n.z):
        start(code.at[lax.rem(z + k, 2)], zbuf.at[:, z], z_send.at[k], z_recv.at[k], z_peer(k))

    loads[1].wait()
    packed = n.layers * 2 * n.groups

    def lane_groups():
        for h in range(2):
            for g in range(2 * n.groups):
                at_lane = h * n.half + g * LANES
                yield slice(at_lane, at_lane + LANES), pl.ds(h * packed + g, n.layers, stride=2 * n.groups), h, g

    for here, spread, _, _ in lane_groups():
        dense[spread, :] = base[:, here].astype(f32) - loc[:, here].astype(f32)
    delta[...] = dense[...].astype(bf16).reshape(delta.shape)

    start(delta.at[1 - mine], pair, d_send.at[0], d_recv.at[0], sibling)

    def token_copy(i):
        there = tok.at[i, n.tokens : 2 * n.tokens]
        return copy(stage.at[i], there, t_send.at[i], t_recv.at[i], partner)

    token_copies = [token_copy(i) for i in range(2 * n.chunks)]
    for i in range(2 * n.chunks):
        loads[3 + 2 * i].wait()

    def send_tokens():
        for c in token_copies:
            c.start()

    pl.when(late == 0)(send_tokens)

    held = lax.broadcasted_iota(jnp.int32, (n.rows, 1), 0)
    xb, yb, zb = (size.bit_length() - 1 for size in (n.x, n.y, n.z))
    wanted = (((held >> zb) & (n.x - 1)) << (yb + zb)) | ((held >> (xb + zb)) << zb) | (held & (n.z - 1))
    spot = lax.broadcasted_iota(jnp.int32, (n.rows, n.rows), 1)
    order[...] = jnp.where(wanted == spot, 1.0, 0.0).astype(bf16)

    copy(pair, pair, d_send.at[0], d_recv.at[0], sibling).wait_recv()
    cross[0] = (delta[mine].astype(f32) + pair[...].astype(f32)).astype(bf16)

    far_copy = copy(cross.at[0], cross.at[1], d_send.at[1], d_recv.at[1], far)

    @pl.when(late == 1)
    def _():
        far_copy.start()
        send_tokens()

    for b in range(n.batches):
        deep = slice(b * n.z // n.batches, (b + 1) * n.z // n.batches)
        for slot in range(deep.start, deep.stop):

            @pl.when(z != slot)
            def _():
                k = lax.rem(z - slot + n.z, n.z)
                copy(zbuf.at[:, slot], zbuf.at[:, slot], z_send.at[k], z_recv.at[k], sibling).wait_recv()

        lines = ((x, n.x, x_peer), (y, n.y, y_peer))
        for part, (place, count, peer) in enumerate(lines):
            for k in sorted(range(1, count), key=lambda k: -min(k, count - k)):
                to = plane.at[part, place, deep]
                start(zbuf.at[part, deep], to, p_send.at[part], p_recv.at[part], peer(k), False)
    rings = ((ring_a, y, n.y, y_peer, x, n.x), (ring_b, x, n.x, x_peer, y, n.y))

    def block_rows(part):
        return rings[part][5] * n.z

    def hop(part, c, way, distance, length, inward):
        ring, p, size, peer, _, _ = rings[part]
        rows = block_rows(part)
        away = distance if inward else distance - length
        block = lax.rem(p + (size - away if way == 0 else away), size)
        cut = pl.ds(0, rows)
        if distance == size // 2:
            cut = pl.ds(0, rows // 2) if way == 0 else pl.ds(rows // 2, rows // 2)
        sems = (r_send.at[part, c, way, distance - 1], r_recv.at[part, c, way, distance - 1])
        slot = ring.at[c, block, cut]
        return copy(slot, slot, *sems, peer(length if way == 0 else size - length))

    def go(part, c, way, distance, length):
        sent.append(hop(part, c, way, distance, length, False))
        sent[-1].start()

    def arrived(part, c, way, distance):
        hop(part, c, way, distance, 1, True).wait_recv()

    for part in range(2):
        ring, p, _, _, other, count = rings[part]
        others = plane.at[part, 0 : count - 1]
        gathered = copy(others, others, p_send.at[part], p_recv.at[part], sibling)
        gathered.wait_recv()
        sent.append(gathered)
        plane[part, other] = zbuf[part]
        rows = block_rows(part)
        wide[0 : rows * n.groups, :] = plane[part, 0:count].reshape(rows * n.groups, LANES).astype(f32)
        per = n.cols // LANES
        for c in range(n.chunks):
            for i in range(per):
                ring[c, p, :, i * LANES : (i + 1) * LANES] = wide[
                    pl.ds(c * per + i, rows, stride=n.groups), :
                ].astype(bf16)
            for distance in FIRST[rings[part][2]]:
                for way in range(2):
                    go(part, c, way, distance, distance)

    @pl.when(late == 0)
    def _():
        pl.semaphore_wait(far_in, 1)
        far_copy.start()

    sent.append(far_copy)

    outer_copy = copy(outer.at[mine], outer.at[mine], d_send.at[2], d_recv.at[2], sibling)

    def average():
        copy(cross.at[1], cross.at[1], d_send.at[1], d_recv.at[1], far).wait_recv()
        outer[mine] = ((cross[0].astype(f32) + cross[1].astype(f32)) / 4.0).astype(bf16)
        outer_copy.start()

    for c in range(n.chunks):
        for part in range(2):
            if rings[part][2] == 8:
                for way in range(2):
                    arrived(part, c, way, 2)
                    go(part, c, way, 3, 1)
                    go(part, c, way, 4, 2)
    average()
    sent.append(outer_copy)
    copy(outer.at[1 - mine], outer.at[1 - mine], d_send.at[2], d_recv.at[2], sibling).wait_recv()
    loads[2].wait()
    dense[...] = outer[...].reshape(dense.shape).astype(f32)
    for here, spread, h, g in lane_groups():
        strided = pl.ds(h * 2 * n.groups + g, n.layers, stride=n.lanes)
        grad = dense[spread, :]
        moved = 0.9 * mom[strided, :] + grad
        mom_out[strided, :] = moved
        new_base = (base[:, here].astype(f32) - 0.7 * (grad + 0.9 * moved)).astype(bf16)
        base_out[:, here] = new_base
        local_out[:, here] = (0.5 * loc[:, here].astype(f32) + 0.5 * new_base.astype(f32)).astype(bf16)

    for i in range(2 * n.chunks):
        loads[4 + 2 * i].wait()

    def product(part, c):
        size = rings[part][2]
        for distance in range(1, size // 2 + 1):
            if not (size == 8 and distance == 2):
                for way in range(2):
                    arrived(part, c, way, distance)
        i = part * n.chunks + c
        token_copy(i).wait_recv()
        return lax.dot_general(
            tok[i],
            rings[part][0][c].reshape(n.rows, n.cols),
            NT,
            preferred_element_type=f32,
        )

    def turn(a):
        high = a.astype(bf16)
        low = (a - high.astype(f32)).astype(bf16)
        return sum(jnp.dot(half, order[...], preferred_element_type=f32) for half in (high, low))

    first_sum = product(0, 0)
    for c in range(1, n.chunks):
        first_sum += product(0, c)
    total = turn(first_sum)
    for c in range(n.chunks):
        total += product(1, c)
    give[...] = total[n.tokens :].astype(bf16)
    start(give, take, g_send, g_recv, partner)
    flush(1)

    copy(give, take, g_send, g_recv, partner).wait_recv()
    proj_out[...] = ((total[: n.tokens] + take[...].astype(f32)) * (1.0 / math.sqrt(n.width))).astype(bf16)
    flush()
    for c in token_copies:
        c.wait_send()


def build(n, tokens, local, base, momentum):
    bf16, f32 = jnp.bfloat16, jnp.float32
    most = max(n.x, n.y)
    dma = pltpu.SemaphoreType.DMA
    packed = n.layers * 2 * n.groups
    arrays = [pltpu.with_memory_space_constraint(a, pltpu.HBM) for a in (tokens, local, base, momentum)]
    return pl.pallas_call(
        functools.partial(kernel, n),
        out_shape=(
            pltpu.VMEM((n.tokens, n.rows), bf16),
            pltpu.VMEM((n.layers, n.width), bf16),
            pltpu.VMEM((n.layers * n.lanes, LANES), f32),
            pltpu.VMEM((n.layers, n.width), bf16),
        ),
        in_specs=[pl.BlockSpec(memory_space=pl.ANY)] * 4,
        out_specs=(pl.BlockSpec(memory_space=pltpu.VMEM),) * 4,
        scratch_shapes=[
            pltpu.VMEM((2 * n.chunks, 2 * n.tokens, n.cols), bf16),
            pltpu.VMEM((2 * n.chunks, n.tokens, n.cols), bf16),
            pltpu.VMEM((n.layers, n.width), bf16),
            pltpu.VMEM((n.layers, n.width), bf16),
            pltpu.VMEM((n.layers * n.lanes, LANES), f32),
            pltpu.VMEM((n.layers * n.lanes, LANES), f32),
            pltpu.VMEM((n.lanes, LANES), f32),
            pltpu.VMEM((2, 2, n.groups, LANES), bf16),
            pltpu.VMEM((2, n.z, n.groups, LANES), bf16),
            pltpu.VMEM((2, most, n.z, n.groups, LANES), bf16),
            pltpu.VMEM((most * n.z * n.groups, LANES), f32),
            pltpu.VMEM((n.chunks, n.y, n.x * n.z, n.cols), bf16),
            pltpu.VMEM((n.chunks, n.x, n.y * n.z, n.cols), bf16),
            pltpu.VMEM((n.rows, n.rows), bf16),
            pltpu.VMEM((n.tokens, n.rows), bf16),
            pltpu.VMEM((n.tokens, n.rows), bf16),
            pltpu.VMEM((2, packed, LANES), bf16),
            pltpu.VMEM((packed, LANES), bf16),
            pltpu.VMEM((2, packed, LANES), bf16),
            pltpu.VMEM((2, packed, LANES), bf16),
            dma((3 + 4 * n.chunks,)),
            pltpu.SemaphoreType.REGULAR,
            dma((2 * n.chunks,)),
            dma((2 * n.chunks,)),
            dma((n.z,)),
            dma((n.z,)),
            dma((2,)),
            dma((2,)),
            dma((2, n.chunks, 2, most // 2)),
            dma((2, n.chunks, 2, most // 2)),
            dma((3,)),
            dma((3,)),
            dma,
            dma,
        ],
        compiler_params=pltpu.CompilerParams(collective_id=0, has_side_effects=True, vmem_limit_bytes=40 * MIB),
    )(*arrays)


def store_kernel(*refs):
    copies = [pltpu.make_async_copy(refs[i], refs[4 + i], refs[8].at[i]) for i in range(4)]
    for one in copies:
        one.start()
    for one in copies:
        one.wait()


def store(*arrays):
    return pl.pallas_call(
        store_kernel,
        out_shape=tuple(jax.ShapeDtypeStruct(a.shape, a.dtype) for a in arrays),
        in_specs=[pl.BlockSpec(memory_space=pltpu.VMEM)] * 4,
        out_specs=(pl.BlockSpec(memory_space=pl.ANY),) * 4,
        scratch_shapes=[pltpu.SemaphoreType.DMA((4,))],
        compiler_params=pltpu.CompilerParams(vmem_limit_bytes=8 * MIB),
    )(*arrays)


def on_device(n, tokens, local_weights, base_weights, momentum):
    projected, new_base, new_momentum, new_local = store(
        *build(
            n,
            tokens.reshape(n.tokens, n.width),
            local_weights.reshape(n.layers, n.width),
            base_weights.reshape(n.layers, n.width),
            momentum.reshape(n.layers * n.lanes, LANES),
        )
    )
    return (
        projected[None],
        new_base.reshape(base_weights.shape),
        new_momentum.reshape(momentum.shape),
        new_local.reshape(local_weights.shape),
    )


def solution(mesh, n=Sizes(8, 8, 4, 8192, 10, 128, 1)):
    return jax.shard_map(
        functools.partial(on_device, n),
        mesh=mesh,
        in_specs=(
            P("rep", "fsdp", None),
            P("rep", None, "fsdp", None),
            P(None, "fsdp", None),
            P(None, "fsdp", None),
        ),
        out_specs=(
            P("rep", "fsdp", None),
            P(None, "fsdp", None),
            P(None, "fsdp", None),
            P("rep", None, "fsdp", None),
        ),
        check_vma=False,
    )
```
